256 devices in a mesh: span: 64 (over x, z, core), mp: 4 (over y).
Axes of the slice: x: 4, y: 4, z: 8, core: 2. Of those that a mesh axis runs over, the one named last changes fastest.
Arguments:
- queries: bfloat16 [32768, 4096], P('span', 'mp'), may hold values from -6 to 6
- grad_out: bfloat16 [32768, 4096], P('span', 'mp'), may hold values from -0.59765625 to 0.59765625
- read_kv: bfloat16 [64, 896, 2, 1024], P('span', None, None, 'mp'), may hold values from -6 to 6
- read_ids: int32 [64, 28], P('span'), may hold values from 0 to 63, all different within a row
- read_counts: int32 [64, 28], P('span'), may hold values from 1 to 512
- gist_states: bfloat16 [2048, 4096], P('span'), may hold values from -16 to 16
- kv_weight: bfloat16 [4096, 2, 1024], P(None, None, 'mp'), may hold values from -0.09375 to 0.09375
Outputs:
- query_grad: bfloat16 [32768, 4096], P('span', 'mp')
- kv_weight_grad: float32 [4096, 2, 1024], P('span', None, 'mp')
- gist_state_grad: bfloat16 [2048, 4096], P('span', 'mp')
The draws below stay inside these ranges and needn't reach their ends.
Inputs may be any that keep to these rules, and one draw needn't show every extreme that they name: `read_ids`: each span reads 28 different spans; every span is read by some span.
All inputs are finite; a program needn't handle non-finite values.
Results may differ from the reference program's by a relative error of at most 0.019.
Values may be sent and summed in bfloat16 or wider, within the bound.
A program may use at most 128 MiB of HBM per device.

```python
import jax
import jax.numpy as jnp
from jax import lax

D = 4096
HQ = 32
KVH = 8
HD = 128
G = 32
LEN = 512
NRC = 28
SPANS = 64
TOKENS = 32768


def draw_read_counts(key, part):
    key = jax.random.fold_in(key, 7)
    first, second = jax.random.split(key)
    values = jax.random.randint(first, (SPANS * NRC,), 1, LEN + 1, dtype=jnp.int32)
    place = jax.random.randint(second, (), 0, SPANS * NRC, dtype=jnp.int32)
    spots = jnp.arange(SPANS * NRC, dtype=jnp.int32)
    values = jnp.where(spots == place, LEN, values)
    return values.reshape(SPANS, NRC)


def raised(values, own_key, source, target, blocks, factor):
    owner, partner = [(jnp.arange(values.shape[axis_at]) // (values.shape[axis_at] // blocks)).reshape([-1 if axis == axis_at else 1 for axis in range(values.ndim)]) for axis_at in (source, target)]
    chosen = jax.random.permutation(own_key, blocks)[partner]
    strong = (owner == chosen) | (owner == (partner + blocks // 2) % blocks)
    return jnp.where(strong, factor * values, values)


def shard_levels(stream_key, extent, cuts, smallest, top_value):
    loudness = 1.0
    for position, blocks in cuts:
        heights = jax.random.uniform(jax.random.fold_in(jax.random.fold_in(stream_key, 6), position), (blocks,), jnp.float32, smallest / len(cuts), top_value / len(cuts))
        loudness = loudness * jnp.repeat(jnp.exp(heights), extent[position] // blocks).reshape((-1,) + (1,) * (len(extent) - 1 - position))
    return loudness


def different_ones(stream_key, rows, number_of, top, lift):
    ranking = jax.random.permutation(jax.random.fold_in(stream_key, 1), number_of)
    boost = ranking
    for power in range(3):
        boost = boost * boost // number_of
    boost = boost * lift // number_of
    chance = jax.random.randint(jax.random.fold_in(stream_key, 2), (rows, number_of), 0, 4096) + boost
    sure = jax.random.permutation(jax.random.fold_in(stream_key, 3), rows)[jnp.arange(number_of) % rows]
    chance = jnp.where(jnp.arange(rows)[:, None] == sure[None, :], 1 << 14, chance)
    score = chance * number_of + jnp.arange(number_of)
    return lax.top_k(score.astype(jnp.int32), top)[1].astype(jnp.int32)


def normal_values(stream_key, shape, spread, bound, shards=(), kind=jnp.bfloat16):
    loudness = shard_levels(stream_key, shape, shards, -0.22, 0.18) if shards else 1.0
    result = jax.random.normal(stream_key, shape, jnp.float32) * spread * loudness
    return jnp.minimum(jnp.maximum(result, -bound), bound).astype(kind)


def noise_with(key, dims, scale, reach, cuts, heavy, kind=jnp.bfloat16):
    values = scale * jax.random.normal(key, dims, jnp.float32)
    if cuts:
        values = values * shard_levels(key, dims, cuts, -0.22, 0.18)
    return jnp.clip(raised(values, jax.random.fold_in(key, 3), *heavy), -reach, reach).astype(kind)


def setup_inputs(seed: int = 0) -> dict:
    splits = jax.random.split(jax.random.key(seed), 8)
    return {
        "queries": normal_values(splits[0], (TOKENS, HQ * HD), 1.0, 6.0, ((0, 64), (1, 4))),
        "grad_out": normal_values(splits[1], (TOKENS, HQ * HD), 0.1, 0.59765625, ((0, 64), (1, 4))),
        "read_kv": normal_values(splits[2], (SPANS, NRC * G, 2, KVH * HD), 1.0, 6.0, ((0, 64), (3, 4))),
        "read_ids": different_ones(splits[3], SPANS, SPANS, NRC, 7168),
        "read_counts": draw_read_counts(jax.random.fold_in(splits[7], 71), 0),
        "gist_states": noise_with(splits[5], (SPANS * G, D), 1.0, 16.0, ((0, 64),), (0, 1, 64, 4.0)),
        "kv_weight": normal_values(splits[6], (D, 2, KVH * HD), D ** -0.5, 0.09375, ((2, 4),)),
    }


def span_backward(query_rows, grad_rows, kv_rows, count_row, groups, gist, operand_type):
    length = query_rows.shape[0]
    key_rows = kv_rows.shape[0]
    kv_width = kv_rows.shape[2]
    kv_heads = kv_width // HD
    scale = HD ** -0.5
    query = query_rows.astype(operand_type).reshape(length, kv_heads, groups, HD)
    upstream = grad_rows.astype(operand_type).reshape(length, kv_heads, groups, HD)
    keys = kv_rows[:, 0, :].astype(operand_type).reshape(key_rows, kv_heads, HD)
    values = kv_rows[:, 1, :].astype(operand_type).reshape(key_rows, kv_heads, HD)
    scores = jnp.einsum("ikgd,jkd->kgij", query, keys, preferred_element_type=jnp.float32) * scale - 1.0
    limits = length - jnp.repeat(count_row, gist)
    visible = jnp.arange(length, dtype=jnp.int32)[:, None] >= limits[None, :]
    sig = jax.nn.sigmoid(scores)
    probs = jnp.where(visible, sig, 0.0).astype(jnp.bfloat16)
    value_part = jnp.einsum("kgij,ikgd->jkd", probs.astype(operand_type), upstream, preferred_element_type=jnp.float32)
    dprob = jnp.einsum("ikgd,jkd->kgij", upstream, values, preferred_element_type=jnp.float32)
    dscore = jnp.where(visible, dprob * sig * (1.0 - sig) * scale, 0.0).astype(jnp.bfloat16)
    key_part = jnp.einsum("kgij,ikgd->jkd", dscore.astype(operand_type), query, preferred_element_type=jnp.float32)
    query_grad = jnp.einsum("kgij,jkd->ikgd", dscore.astype(operand_type), keys, preferred_element_type=jnp.float32)
    query_grad = query_grad.astype(jnp.bfloat16).reshape(length, kv_heads * groups * HD)
    parts = jnp.stack([key_part.reshape(key_rows, kv_width), value_part.reshape(key_rows, kv_width)], axis=1)
    return query_grad, parts


def reference(queries, grad_out, read_kv, read_ids, read_counts, gist_states, kv_weight):
    groups = HQ // KVH
    kv_width = KVH * HD
    query_blocks = queries.reshape(SPANS, LEN, HQ * HD)
    grad_blocks = grad_out.reshape(SPANS, LEN, HQ * HD)

    def one_span(items):
        return span_backward(items[0], items[1], items[2], items[3], groups, G, jnp.float32)

    query_grad, parts = lax.map(one_span, (query_blocks, grad_blocks, read_kv, read_counts))
    flat_parts = parts.reshape(SPANS * NRC, G * 2 * kv_width)
    gist_sum = jax.ops.segment_sum(flat_parts, read_ids.reshape(-1), num_segments=SPANS)
    gist_grad = gist_sum.astype(jnp.bfloat16).reshape(SPANS * G, 2 * kv_width)
    weight_grad = jnp.dot(gist_states.T, gist_grad, preferred_element_type=jnp.float32).reshape(D, 2, kv_width)
    state_grad = jnp.dot(gist_grad, kv_weight.reshape(D, 2 * kv_width).T, preferred_element_type=jnp.float32)
    return query_grad.reshape(TOKENS, HQ * HD), weight_grad, state_grad.astype(jnp.bfloat16)
```

```python
import jax
import jax.numpy as jnp
from jax import lax
from jax.experimental import pallas as pl
from jax.experimental.pallas import tpu as pltpu
from jax.sharding import PartitionSpec as P

HD = 128
SLOTS = 28
G = 32
LEN = 512
ROWS = SLOTS * G
NX, NZ, NY = 4, 8, 4
TILE = 128
SCALE = HD ** (-0.5)
NT = (((1,), (1,)), ((), ()))
NN = (((1,), (0,)), ((), ()))
MESH = pl.DeviceIdType.MESH
F32, BF16 = jnp.float32, jnp.bfloat16


def dot(a, b, dims=NN):
    return lax.dot_general(a, b, dims, preferred_element_type=F32)


def unmix():
    r = lax.broadcasted_iota(jnp.int32, (256, 256), 0)
    c = lax.broadcasted_iota(jnp.int32, (256, 256), 1)
    return jnp.where(c == jnp.where(r < 128, 2 * r, 2 * r - 255), 1.0, 0.0).astype(BF16)


GS = 0
Y = 7
BASE, PER = 10, 28
CORE, XA, XB, XC, ZR, AG, WC, WX = 0, 4, 6, 8, 10, 17, 24, 25
NREMOTE = BASE + 2 * PER


def kernel(
    pos, cnt, q_hbm, do_hbm, kv_hbm, gs_hbm, w_hbm,
    dq_hbm, wg_ref, sg_ref,
    q_ref, do_ref, kv_ref, gs_ref, w_ref, dq_ref,
    k_s, v_s, kt_s, dk_s, dv_s, ds_s,
    parts, sbuf, rbuf, xs, relay, xr, pz, zr, gg, ggall,
    gsend, gsall, gst, wd, usend, ur, wp, wsend, wr, qsend, qr,
    lsem, ssem, rsem,
):
    span = lax.axis_index("span")
    y = lax.axis_index("mp")
    x, z, c = span // (NZ * 2), (span // 2) % NZ, span % 2

    def at(dx=0, dz=0, dc=0, dy=0):
        place = (((x + dx) % NX) * NZ + (z + dz) % NZ) * 2 + (c + dc) % 2
        return {"span": place, "mp": (y + dy) % NY}

    def remote(src, dst, k, to):
        return pltpu.make_async_remote_copy(
            src_ref=src, dst_ref=dst, send_sem=ssem.at[k], recv_sem=rsem.at[k],
            device_id=to, device_id_type=MESH,
        )

    loads = [pltpu.make_async_copy(kv_hbm.reshape(2 * ROWS, 256), kv_ref, lsem.at[0])]
    for n, (i, o) in enumerate(((q_hbm, q_ref), (do_hbm, do_ref))):
        loads.append(pltpu.make_async_copy(i, o, lsem.at[1 + n]))
    loads.append(pltpu.make_async_copy(gs_hbm, gs_ref, lsem.at[3]))
    loads.append(pltpu.make_async_copy(w_hbm.reshape(8192, 256), w_ref, lsem.at[4]))
    for load in loads:
        load.start()

    peers = [at(dc=1)] + [at(dx=d) for d in (1, 2, 3)]
    peers += [at(dz=d) for d in range(1, NZ)] + [at(dy=d) for d in (1, 2, 3)]
    barrier = pltpu.get_barrier_semaphore()
    for peer in peers:
        pl.semaphore_signal(barrier, inc=1, device_id=peer, device_id_type=MESH)

    lane8 = lax.broadcasted_iota(jnp.int32, (8, 128), 1)
    for h in range(2):
        parts[h, SLOTS] = jnp.zeros((G, 256), BF16)
    dk_s[...] = jnp.zeros_like(dk_s)
    dv_s[...] = jnp.zeros_like(dv_s)

    loads[0].wait()
    pm = unmix()
    for b in range(7):
        blk = dot(pm, kv_ref[b * 256 : (b + 1) * 256, :]).astype(BF16)
        for h in range(2):
            kk = blk[:128, h * 128 : (h + 1) * 128]
            k_s[h, b * 128 : (b + 1) * 128, :] = kk
            v_s[h, b * 128 : (b + 1) * 128, :] = blk[128:, h * 128 : (h + 1) * 128]
            kt_s[h, :, b * 128 : (b + 1) * 128] = kk.T

    loads[3].wait()
    for zt in range(NZ):
        for xt in range(NX):
            col = (xt * NZ + zt) * 128
            gsend[zt, :, xt * 128 : (xt + 1) * 128] = gs_ref[:, col : col + 128]
    gsall[pl.ds(pl.multiple_of(z * G, G), G), :] = gsend[z]
    pl.semaphore_wait(barrier, len(peers))

    def gs_copy(d):
        rows = pl.ds(pl.multiple_of(z * G, G), G)
        return remote(gsend.at[(z + d) % NZ], gsall.at[rows], GS + d - 1, at(dz=d))

    for d in (4, 3, 5, 2, 6, 1, 7):
        gs_copy(d).start()
    loads[1].wait()
    loads[2].wait()

    def tile_rows(ref, h, t):
        tok = pl.ds(pl.multiple_of(t * TILE, TILE), TILE)
        return jnp.concatenate(
            [ref[tok, pl.ds(pl.multiple_of(h * 512 + g * 128, 128), 128)] for g in range(4)], axis=0
        )

    def attend(i):
        h, t = i // 4, i % 4
        qt, dt = tile_rows(q_ref, h, t), tile_rows(do_ref, h, t)
        s = dot(k_s[h], qt, NT)
        dp = dot(v_s[h], dt, NT)
        bias = []
        for j in range(SLOTS):
            first = LEN - cnt[0, j] - t * TILE
            row = jnp.where(lane8 >= first, -0.5, -1e30).astype(F32)
            bias.append(jnp.concatenate([jnp.concatenate([row] * 4, axis=1)] * 4, axis=0))
        u = jnp.tanh(s * (0.5 * SCALE) + jnp.concatenate(bias, axis=0))
        probs = (0.5 + 0.5 * u).astype(BF16)
        ds = (dp * (1.0 - u * u)).astype(BF16)
        ds_s[i] = ds
        dv_s[h] += dot(probs, dt)
        dk_s[h] += dot(ds, qt)

    def finish_dq(i):
        h, t = i // 4, i % 4
        tok = pl.ds(pl.multiple_of(t * TILE, TILE), TILE)
        dqt = dot(kt_s[h], ds_s[i]) * (0.25 * SCALE)
        for g in range(4):
            cols = pl.ds(pl.multiple_of(h * 512 + g * 128, 128), 128)
            dq_ref[tok, cols] = dqt[:, g * 128 : (g + 1) * 128].T.astype(BF16)

    def block(k):
        return pl.ds(pl.multiple_of(k * G, G), G)

    def core_copy(h, d):
        return remote(sbuf.at[h, d], rbuf.at[h, d], BASE + PER * h + CORE + d, at(dc=1))

    def core_send(h):
        parts[h, :SLOTS, :, :128] = (dk_s[h] * (0.25 * SCALE)).astype(BF16).reshape(SLOTS, G, 128)
        parts[h, :SLOTS, :, 128:] = dv_s[h].astype(BF16).reshape(SLOTS, G, 128)
        for d in (2, 1, 3, 0):
            def gather(zt, carry):
                p = pos[0, (((x + d) % NX) * NZ + zt) * 2 + 1 - c]
                sbuf[h, d, block(zt), :] = parts[h, p]
                return carry
            lax.fori_loop(0, NZ, gather, 0)
            core_copy(h, d).start()

    def pair_sum(h, d):
        core_copy(h, d).wait_recv()
        def add(zt, carry):
            p = pos[0, (((x + d) % NX) * NZ + zt) * 2 + c]
            own = parts[h, p].astype(F32)
            xs[h, d, block(zt), :] = (own + rbuf[h, d, block(zt), :].astype(F32)).astype(BF16)
            return carry
        lax.fori_loop(0, NZ, add, 0)

    LO, HI = pl.ds(0, 128), pl.ds(128, 128)

    def xa(h, n):
        rows = (LO, HI)[n]
        return remote(xs.at[h, 2, rows], relay.at[h, n], BASE + PER * h + XA + n, at(dx=(1, 3)[n]))

    def xb(h, n):
        d, rows = ((1, HI), (3, LO))[n]
        return remote(xs.at[h, d, rows], xr.at[h, n, rows], BASE + PER * h + XB + n, at(dx=d))

    def xc(h, n):
        d, rows = ((1, LO), (3, HI))[n]
        return remote(xs.at[h, d, rows], xr.at[h, n, rows], BASE + PER * h + XC + n, at(dx=d))

    def x_first(h):
        pair_sum(h, 2)
        xa(h, 0).start()
        xa(h, 1).start()
        pair_sum(h, 1)
        xb(h, 0).start()
        pair_sum(h, 3)
        xb(h, 1).start()
        pair_sum(h, 0)

    def x_second(h):
        for n in range(2):
            d, rows = ((1, slice(0, 128)), (3, slice(128, 256)))[n]
            xa(h, n).wait_recv()
            xs[h, d, rows, :] = (xs[h, d, rows, :].astype(F32) + relay[h, n].astype(F32)).astype(BF16)
            xc(h, n).start()

    def z_copy(h, d):
        return remote(pz.at[h, block((z + d) % NZ)], zr.at[h, d - 1], BASE + PER * h + ZR + d - 1, at(dz=d))

    def z_send(h):
        for n in range(2):
            xb(h, n).wait_recv()
            xc(h, n).wait_recv()
        pz[h] = (xs[h, 0].astype(F32) + xr[h, 0].astype(F32) + xr[h, 1].astype(F32)).astype(BF16)
        for d in (4, 3, 5, 2, 6, 1, 7):
            z_copy(h, d).start()

    def ag_copy(h, d):
        return remote(gg.at[h], ggall.at[h, block(z)], BASE + PER * h + AG + d - 1, at(dz=d))

    def z_sum(h):
        total = pz[h, block(z), :].astype(F32)
        for d in range(1, NZ):
            z_copy(h, d).wait_recv()
            total += zr[h, d - 1].astype(F32)
        gg[h] = total.astype(BF16)
        for d in (4, 3, 5, 2, 6, 1, 7):
            ag_copy(h, d).start()
        ggall[h, block(z), :] = gg[h]

    def wc_copy(h):
        return remote(wsend.at[h], wr.at[h], BASE + PER * h + WC, at(dc=1))

    def wx_copy(h, d):
        return remote(qsend.at[h, d - 1], qr.at[h, d - 1], BASE + PER * h + WX + d - 1, at(dx=d))

    def rows_of(xt, cc):
        return pl.ds(pl.multiple_of(xt * 128 + cc * 64, 64), 64)

    def w_first(h):
        for d in range(1, NZ):
            ag_copy(h, d).wait_recv()
        wp[h] = dot(gst[...], ggall[h])
        for xt in range(NX):
            wsend[h, xt] = wp[h, rows_of(xt, 1 - c), :].astype(BF16)
        wc_copy(h).start()

    def w_second(h):
        wc_copy(h).wait_recv()
        for d in (2, 1, 3):
            xt = (x + d) % NX
            qsend[h, d - 1] = (wp[h, rows_of(xt, c), :] + wr[h, xt].astype(F32)).astype(BF16)
            wx_copy(h, d).start()

    def w_last(h):
        total = wp[h, rows_of(x, c), :] + wr[h, x].astype(F32)
        for d in (1, 2, 3):
            wx_copy(h, d).wait_recv()
            total += qr[h, d - 1].astype(F32)
        for s in range(2):
            wg_ref[:, s, h * 128 : (h + 1) * 128] = total[:, s * 128 : (s + 1) * 128]

    def y_copy(d):
        return remote(usend.at[(y + d) % NY], ur.at[d - 1], Y + d - 1, at(dy=d))

    def state_send():
        for yt in range(NY):
            rows = slice(yt * 1024, (yt + 1) * 1024)
            part = jnp.zeros((G, 1024), F32)
            for s in range(2):
                left = jnp.concatenate([gg[h, :, s * 128 : (s + 1) * 128] for h in range(2)], axis=1)
                part += dot(left, wd[s, rows, :], NT)
            usend[yt] = part.astype(BF16)
        for d in (2, 1, 3):
            y_copy(d).start()

    def state_last():
        total = usend[y].astype(F32)
        for d in (1, 2, 3):
            y_copy(d).wait_recv()
            total += ur[d - 1].astype(F32)
        sg_ref[...] = total.astype(BF16)

    def loop(i, carry):
        attend(i)
        pl.when(i == 3)(lambda: core_send(0))
        pl.when(i == 4)(lambda: x_first(0))
        pl.when(i == 5)(lambda: x_second(0))
        pl.when(i == 6)(lambda: z_send(0))
        return carry

    lax.fori_loop(0, 8, loop, 0)

    def dq_steps(lo, hi):
        lax.fori_loop(lo, hi, lambda i, carry: (finish_dq(i), carry)[1], 0)

    core_send(1)
    z_sum(0)
    x_first(1)
    for d in range(1, NZ):
        gs_copy(d).wait_recv()
    gst[...] = gsall[...].T
    dq_steps(0, 4)
    x_second(1)
    loads[4].wait()

    def split_w(b, carry):
        blk = dot(pm, w_ref[pl.ds(pl.multiple_of(b * 256, 256), 256), :]).astype(BF16)
        rows = pl.ds(pl.multiple_of(b * 128, 128), 128)
        wd[0, rows, :] = blk[:128]
        wd[1, rows, :] = blk[128:]
        return carry

    lax.fori_loop(0, 32, split_w, 0)
    z_send(1)
    dq_steps(4, 8)
    dq_out = pltpu.make_async_copy(dq_ref, dq_hbm, lsem.at[6])
    dq_out.start()
    w_first(0)
    w_second(0)
    z_sum(1)
    state_send()
    w_last(0)
    w_first(1)
    w_second(1)
    state_last()
    w_last(1)

    dq_out.wait()
    for d in range(1, NZ):
        gs_copy(d).wait_send()
    for d in (1, 2, 3):
        y_copy(d).wait_send()
    for h in range(2):
        for d in range(4):
            core_copy(h, d).wait_send()
        for n in range(2):
            xa(h, n).wait_send()
            xb(h, n).wait_send()
            xc(h, n).wait_send()
        for d in range(1, NZ):
            z_copy(h, d).wait_send()
            ag_copy(h, d).wait_send()
        wc_copy(h).wait_send()
        for d in (1, 2, 3):
            wx_copy(h, d).wait_send()


def body(queries, grad_out, read_kv, read_ids, read_counts, gist_states, kv_weight):
    smem, vmem, anywhere = (pl.BlockSpec(memory_space=m) for m in (pltpu.SMEM, pltpu.VMEM, pl.ANY))
    scratch = [
        ((512, 1024), BF16), ((512, 1024), BF16), ((2 * ROWS, 256), BF16), ((G, 4096), BF16),
        ((8192, 256), BF16), ((512, 1024), BF16),
        ((2, ROWS, 128), BF16), ((2, ROWS, 128), BF16), ((2, 128, ROWS), BF16),
        ((2, ROWS, 128), F32), ((2, ROWS, 128), F32), ((8, ROWS, 512), BF16),
    ]
    scratch2 = [
        ((2, SLOTS + 1, G, 256), BF16), ((2, 4, 256, 256), BF16), ((2, 4, 256, 256), BF16), ((2, 4, 256, 256), BF16),
        ((2, 2, 128, 256), BF16), ((2, 2, 256, 256), BF16), ((2, 256, 256), BF16), ((2, 7, G, 256), BF16),
        ((2, G, 256), BF16), ((2, 256, 256), BF16),
        ((NZ, G, 512), BF16), ((256, 512), BF16), ((512, 256), BF16), ((2, 4096, 256), BF16),
        ((NY, G, 1024), BF16), ((3, G, 1024), BF16), ((2, 512, 256), F32), ((2, NX, 64, 256), BF16),
        ((2, NX, 64, 256), BF16), ((2, 3, 64, 256), BF16), ((2, 3, 64, 256), BF16),
    ]
    spans = jnp.arange(NX * NZ * 2, dtype=jnp.int32)
    slots = jnp.arange(SLOTS, dtype=jnp.int32)
    found = read_ids[0][None, :] == spans[:, None]
    pos = jnp.min(jnp.where(found, slots[None, :], SLOTS), axis=1)[None, :]
    return pl.pallas_call(
        kernel,
        out_shape=(
            jax.ShapeDtypeStruct((512, 1024), BF16),
            jax.ShapeDtypeStruct((64, 2, 256), F32),
            jax.ShapeDtypeStruct((G, 1024), BF16),
        ),
        in_specs=[smem, smem] + [anywhere] * 5,
        out_specs=(anywhere, vmem, vmem),
        scratch_shapes=[pltpu.VMEM(*s) for s in scratch]
        + [pltpu.VMEM(*s) for s in scratch2]
        + [pltpu.SemaphoreType.DMA((7,)), pltpu.SemaphoreType.DMA((NREMOTE,)), pltpu.SemaphoreType.DMA((NREMOTE,))],
        compiler_params=pltpu.CompilerParams(
            collective_id=0, has_side_effects=True, vmem_limit_bytes=60 * 2**20
        ),
        cost_estimate=pl.CostEstimate(flops=5_000_000_000, bytes_accessed=9_000_000, transcendentals=3_670_016),
        name="gist_backward",
    )(pos, read_counts, queries, grad_out, read_kv.reshape(ROWS, 2, 256), gist_states, kv_weight)


def solution(mesh):
    placed = (
        P("span", "mp"),
        P("span", "mp"),
        P("span", None, None, "mp"),
        P("span", None),
        P("span", None),
        P("span", None),
        P(None, None, "mp"),
    )
    return jax.shard_map(
        body,
        mesh=mesh,
        in_specs=placed,
        out_specs=(P("span", "mp"), P("span", None, "mp"), P("span", "mp")),
        check_vma=False,
    )
```

```python
import jax
import jax.numpy as jnp
from jax import lax
from jax.experimental import pallas as pl
from jax.experimental.pallas import tpu as pltpu
from jax.sharding import PartitionSpec as P

HD = 128
SLOTS = 28
G = 32
LEN = 512
ROWS = SLOTS * G
NX, NZ, NY = 4, 8, 4
TILE = 128
SCALE = HD ** (-0.5)
NT = (((1,), (1,)), ((), ()))
NN = (((1,), (0,)), ((), ()))
MESH = pl.DeviceIdType.MESH
F32, BF16 = jnp.float32, jnp.bfloat16


def dot(a, b, dims=NN):
    return lax.dot_general(a, b, dims, preferred_element_type=F32)


def unmix():
    r = lax.broadcasted_iota(jnp.int32, (256, 256), 0)
    c = lax.broadcasted_iota(jnp.int32, (256, 256), 1)
    return jnp.where(c == jnp.where(r < 128, 2 * r, 2 * r - 255), 1.0, 0.0).astype(BF16)


GS = 0
Y = 7
BASE, PER = 10, 28
CORE, XA, XB, XC, ZR, AG, WC, WX = 0, 4, 6, 8, 10, 17, 24, 25
NREMOTE = BASE + 2 * PER


def kernel(
    ids, cnt, q_hbm, do_hbm, kv_hbm, gs_hbm, w_hbm,
    dq_ref, wg_ref, sg_ref,
    q_ref, do_ref, kv_ref, gs_ref, w_ref,
    k_s, v_s, kt_s, dk_s, dv_s, ds_s, posv, pos,
    parts, sbuf, rbuf, xs, relay, xr, pz, zr, gg, ggall,
    gsend, gsall, gst, wd, usend, ur, wp, wsend, wr, qsend, qr,
    lsem, ssem, rsem,
):
    span = lax.axis_index("span")
    y = lax.axis_index("mp")
    x, z, c = span // (NZ * 2), (span // 2) % NZ, span % 2

    def at(dx=0, dz=0, dc=0, dy=0):
        place = (((x + dx) % NX) * NZ + (z + dz) % NZ) * 2 + (c + dc) % 2
        return {"span": place, "mp": (y + dy) % NY}

    def remote(src, dst, k, to):
        return pltpu.make_async_remote_copy(
            src_ref=src, dst_ref=dst, send_sem=ssem.at[k], recv_sem=rsem.at[k],
            device_id=to, device_id_type=MESH,
        )

    sent, got = [], []

    def start(copy, *which):
        copy(*which).start()
        sent.append((copy, which))

    def arrived(copy, *which):
        copy(*which).wait_recv()
        got.append((copy, which))

    loads = [pltpu.make_async_copy(kv_hbm.reshape(2 * ROWS, 256), kv_ref, lsem.at[0])]
    for n, (i, o) in enumerate(((q_hbm, q_ref), (do_hbm, do_ref))):
        loads.append(pltpu.make_async_copy(i, o, lsem.at[1 + n]))
    loads.append(pltpu.make_async_copy(gs_hbm, gs_ref, lsem.at[3]))
    loads.append(pltpu.make_async_copy(w_hbm.reshape(8192, 256), w_ref, lsem.at[4]))
    for load in loads[:4]:
        load.start()

    peers = [at(dc=1)] + [at(dx=d) for d in (1, 2, 3)]
    peers += [at(dz=d) for d in range(1, NZ)] + [at(dy=d) for d in (1, 2, 3)]
    barrier = pltpu.get_barrier_semaphore()
    for peer in peers:
        pl.semaphore_signal(barrier, inc=1, device_id=peer, device_id_type=MESH)

    lane8 = lax.broadcasted_iota(jnp.int32, (8, 128), 1)
    where = jnp.full((8, 128), SLOTS, jnp.int32)
    for t in range(SLOTS):
        where = jnp.where(lane8 == ids[0, t], t, where)
    posv[...] = where
    to_smem = pltpu.make_async_copy(posv, pos, lsem.at[5])
    to_smem.start()
    for h in range(2):
        parts[h, SLOTS] = jnp.zeros((G, 256), BF16)
    dk_s[...] = jnp.zeros_like(dk_s)
    dv_s[...] = jnp.zeros_like(dv_s)

    loads[0].wait()
    pm = unmix()
    for b in range(7):
        blk = dot(pm, kv_ref[b * 256 : (b + 1) * 256, :]).astype(BF16)
        for h in range(2):
            kk = blk[:128, h * 128 : (h + 1) * 128]
            k_s[h, b * 128 : (b + 1) * 128, :] = kk
            v_s[h, b * 128 : (b + 1) * 128, :] = blk[128:, h * 128 : (h + 1) * 128]
            kt_s[h, :, b * 128 : (b + 1) * 128] = kk.T

    def gs_copy(d):
        rows = pl.ds(pl.multiple_of(z * G, G), G)
        return remote(gsend.at[(z + d) % NZ], gsall.at[rows], GS + d - 1, at(dz=d))

    def gs_send():
        loads[3].wait()
        for zt in range(NZ):
            for xt in range(NX):
                col = (xt * NZ + zt) * 128
                gsend[zt, :, xt * 128 : (xt + 1) * 128] = gs_ref[:, col : col + 128]
        gsall[pl.ds(pl.multiple_of(z * G, G), G), :] = gsend[z]
        pl.semaphore_wait(barrier, len(peers))
        for d in (4, 3, 5, 2, 6, 1, 7):
            start(gs_copy, d)
        loads[4].start()

    loads[1].wait()
    loads[2].wait()

    def tile_rows(ref, h, t):
        tok = pl.ds(pl.multiple_of(t * TILE, TILE), TILE)
        return jnp.concatenate(
            [ref[tok, pl.ds(pl.multiple_of(h * 512 + g * 128, 128), 128)] for g in range(4)], axis=0
        )

    def attend(i):
        h, t = i // 4, i % 4
        qt, dt = tile_rows(q_ref, h, t), tile_rows(do_ref, h, t)
        s = dot(k_s[h], qt, NT)
        dp = dot(v_s[h], dt, NT)
        bias = []
        for j in range(SLOTS):
            first = LEN - cnt[0, j] - t * TILE
            row = jnp.where(lane8 >= first, -0.5, -1e30).astype(F32)
            bias.append(jnp.concatenate([jnp.concatenate([row] * 4, axis=1)] * 4, axis=0))
        u = jnp.tanh(s * (0.5 * SCALE) + jnp.concatenate(bias, axis=0))
        probs = (0.5 + 0.5 * u).astype(BF16)
        ds = (dp * (1.0 - u * u)).astype(BF16)
        ds_s[i] = ds
        dv_s[h] += dot(probs, dt)
        dk_s[h] += dot(ds, qt)

    def finish_dq(i):
        h, t = i // 4, i % 4
        tok = pl.ds(pl.multiple_of(t * TILE, TILE), TILE)
        dqt = dot(kt_s[h], ds_s[i]) * (0.25 * SCALE)
        for g in range(4):
            cols = pl.ds(pl.multiple_of(h * 512 + g * 128, 128), 128)
            dq_ref[tok, cols] = dqt[:, g * 128 : (g + 1) * 128].T.astype(BF16)

    def block(k):
        return pl.ds(pl.multiple_of(k * G, G), G)

    def core_copy(h, d):
        return remote(sbuf.at[h, d], rbuf.at[h, d], BASE + PER * h + CORE + d, at(dc=1))

    def core_send(h):
        parts[h, :SLOTS, :, :128] = (dk_s[h] * (0.25 * SCALE)).astype(BF16).reshape(SLOTS, G, 128)
        parts[h, :SLOTS, :, 128:] = dv_s[h].astype(BF16).reshape(SLOTS, G, 128)
        for d in (2, 1, 3, 0):
            def gather(zt, carry):
                p = pos[0, (((x + d) % NX) * NZ + zt) * 2 + 1 - c]
                sbuf[h, d, block(zt), :] = parts[h, p]
                return carry
            lax.fori_loop(0, NZ, gather, 0)
            start(core_copy, h, d)

    def pair_sum(h, d):
        arrived(core_copy, h, d)
        def add(zt, carry):
            p = pos[0, (((x + d) % NX) * NZ + zt) * 2 + c]
            own = parts[h, p].astype(F32)
            xs[h, d, block(zt), :] = (own + rbuf[h, d, block(zt), :].astype(F32)).astype(BF16)
            return carry
        lax.fori_loop(0, NZ, add, 0)

    LO, HI = pl.ds(0, 128), pl.ds(128, 128)

    def xa(h, n):
        rows = (LO, HI)[n]
        return remote(xs.at[h, 2, rows], relay.at[h, n], BASE + PER * h + XA + n, at(dx=(1, 3)[n]))

    def xb(h, n):
        d, rows = ((1, HI), (3, LO))[n]
        return remote(xs.at[h, d, rows], xr.at[h, n, rows], BASE + PER * h + XB + n, at(dx=d))

    def xc(h, n):
        d, rows = ((1, LO), (3, HI))[n]
        return remote(xs.at[h, d, rows], xr.at[h, n, rows], BASE + PER * h + XC + n, at(dx=d))

    def x_first(h):
        pair_sum(h, 2)
        start(xa, h, 0)
        start(xa, h, 1)
        pair_sum(h, 1)
        start(xb, h, 0)
        pair_sum(h, 3)
        start(xb, h, 1)
        pair_sum(h, 0)

    def x_second(h):
        for n in range(2):
            d, rows = ((1, slice(0, 128)), (3, slice(128, 256)))[n]
            arrived(xa, h, n)
            xs[h, d, rows, :] = (xs[h, d, rows, :].astype(F32) + relay[h, n].astype(F32)).astype(BF16)
            start(xc, h, n)

    def z_copy(h, d):
        return remote(pz.at[h, block((z + d) % NZ)], zr.at[h, d - 1], BASE + PER * h + ZR + d - 1, at(dz=d))

    def z_send(h):
        for n in range(2):
            arrived(xb, h, n)
            arrived(xc, h, n)
        pz[h] = (xs[h, 0].astype(F32) + xr[h, 0].astype(F32) + xr[h, 1].astype(F32)).astype(BF16)
        for d in (4, 3, 5, 2, 6, 1, 7):
            start(z_copy, h, d)

    def ag_copy(h, d):
        return remote(gg.at[h], ggall.at[h, block(z)], BASE + PER * h + AG + d - 1, at(dz=d))

    def z_sum(h):
        total = pz[h, block(z), :].astype(F32)
        for d in range(1, NZ):
            arrived(z_copy, h, d)
            total += zr[h, d - 1].astype(F32)
        gg[h] = total.astype(BF16)
        for d in (4, 3, 5, 2, 6, 1, 7):
            start(ag_copy, h, d)
        ggall[h, block(z), :] = gg[h]

    def wc_copy(h):
        return remote(wsend.at[h], wr.at[h], BASE + PER * h + WC, at(dc=1))

    def wx_copy(h, d):
        return remote(qsend.at[h, d - 1], qr.at[h, d - 1], BASE + PER * h + WX + d - 1, at(dx=d))

    def rows_of(xt, cc):
        return pl.ds(pl.multiple_of(xt * 128 + cc * 64, 64), 64)

    def w_first(h):
        for d in range(1, NZ):
            arrived(ag_copy, h, d)
        wp[h] = dot(gst[...], ggall[h])
        for xt in range(NX):
            wsend[h, xt] = wp[h, rows_of(xt, 1 - c), :].astype(BF16)
        start(wc_copy, h)

    def w_second(h):
        arrived(wc_copy, h)
        for d in (2, 1, 3):
            xt = (x + d) % NX
            qsend[h, d - 1] = (wp[h, rows_of(xt, c), :] + wr[h, xt].astype(F32)).astype(BF16)
            start(wx_copy, h, d)

    def w_last(h):
        total = wp[h, rows_of(x, c), :] + wr[h, x].astype(F32)
        for d in (1, 2, 3):
            arrived(wx_copy, h, d)
            total += qr[h, d - 1].astype(F32)
        for s in range(2):
            wg_ref[:, s, h * 128 : (h + 1) * 128] = total[:, s * 128 : (s + 1) * 128]

    def y_copy(d):
        return remote(usend.at[(y + d) % NY], ur.at[d - 1], Y + d - 1, at(dy=d))

    def state_send():
        for yt in range(NY):
            rows = slice(yt * 1024, (yt + 1) * 1024)
            part = jnp.zeros((G, 1024), F32)
            for s in range(2):
                left = jnp.concatenate([gg[h, :, s * 128 : (s + 1) * 128] for h in range(2)], axis=1)
                part += dot(left, wd[s, rows, :], NT)
            usend[yt] = part.astype(BF16)
        for d in (2, 1, 3):
            start(y_copy, d)

    def state_last():
        total = usend[y].astype(F32)
        for d in (1, 2, 3):
            arrived(y_copy, d)
            total += ur[d - 1].astype(F32)
        sg_ref[...] = total.astype(BF16)

    def dq_steps(lo, hi):
        lax.fori_loop(lo, hi, lambda i, carry: (finish_dq(i), carry)[1], 0)

    def split_w(lo, hi):
        def one(b, carry):
            blk = dot(pm, w_ref[pl.ds(pl.multiple_of(b * 256, 256), 256), :]).astype(BF16)
            rows = pl.ds(pl.multiple_of(b * 128, 128), 128)
            wd[0, rows, :] = blk[:128]
            wd[1, rows, :] = blk[128:]
            return carry

        lax.fori_loop(lo, hi, one, 0)

    to_smem.wait()

    def loop(i, carry):
        attend(i)

        @pl.when(i == 0)
        def _():
            gs_send()

        @pl.when(i == 3)
        def _():
            core_send(0)

        @pl.when(i == 5)
        def _():
            x_first(0)

        @pl.when(i == 7)
        def _():
            core_send(1)
            x_second(0)

        return carry

    lax.fori_loop(0, 8, loop, 0)

    loads[4].wait()
    split_w(0, 8)
    x_first(1)
    dq_steps(0, 4)
    z_send(0)
    split_w(8, 16)
    x_second(1)
    split_w(16, 32)
    for d in range(1, NZ):
        arrived(gs_copy, d)
    gst[...] = gsall[...].T
    z_send(1)
    z_sum(0)
    dq_steps(4, 8)
    z_sum(1)
    state_send()
    w_first(0)
    w_second(0)
    w_first(1)
    w_last(0)
    w_second(1)
    state_last()
    w_last(1)

    for copy, which in sent:
        copy(*which).wait_send()


def write_out(a, b, c, a_out, b_out, c_out, a_s, b_s, c_s, sem):
    moves = [(a.at[pl.ds(r, 128)], a_s.at[pl.ds(r, 128)], a_out.at[pl.ds(r, 128)]) for r in range(0, 512, 128)]
    moves += [(b, b_s, b_out), (c, c_s, c_out)]
    reads = [pltpu.make_async_copy(i, s, sem.at[0, n]) for n, (i, s, _) in enumerate(moves)]
    writes = [pltpu.make_async_copy(s, o, sem.at[1, n]) for n, (_, s, o) in enumerate(moves)]
    for read in reads:
        read.start()
    for read, write in zip(reads, writes):
        read.wait()
        write.start()
    for write in writes:
        write.wait()


def body(queries, grad_out, read_kv, read_ids, read_counts, gist_states, kv_weight):
    smem, vmem, anywhere = (pl.BlockSpec(memory_space=m) for m in (pltpu.SMEM, pltpu.VMEM, pl.ANY))
    scratch = [
        ((512, 1024), BF16), ((512, 1024), BF16), ((2 * ROWS, 256), BF16), ((G, 4096), BF16),
        ((8192, 256), BF16),
        ((2, ROWS, 128), BF16), ((2, ROWS, 128), BF16), ((2, 128, ROWS), BF16),
        ((2, ROWS, 128), F32), ((2, ROWS, 128), F32), ((8, ROWS, 512), BF16), ((8, 128), jnp.int32),
    ]
    scratch2 = [
        ((2, SLOTS + 1, G, 256), BF16), ((2, 4, 256, 256), BF16), ((2, 4, 256, 256), BF16), ((2, 4, 256, 256), BF16),
        ((2, 2, 128, 256), BF16), ((2, 2, 256, 256), BF16), ((2, 256, 256), BF16), ((2, 7, G, 256), BF16),
        ((2, G, 256), BF16), ((2, 256, 256), BF16),
        ((NZ, G, 512), BF16), ((256, 512), BF16), ((512, 256), BF16), ((2, 4096, 256), BF16),
        ((NY, G, 1024), BF16), ((3, G, 1024), BF16), ((2, 512, 256), F32), ((2, NX, 64, 256), BF16),
        ((2, NX, 64, 256), BF16), ((2, 3, 64, 256), BF16), ((2, 3, 64, 256), BF16),
    ]
    results = pl.pallas_call(
        kernel,
        out_shape=(
            jax.ShapeDtypeStruct((512, 1024), BF16),
            jax.ShapeDtypeStruct((64, 2, 256), F32),
            jax.ShapeDtypeStruct((G, 1024), BF16),
        ),
        in_specs=[smem, smem] + [anywhere] * 5,
        out_specs=(vmem, vmem, vmem),
        scratch_shapes=[pltpu.VMEM(*s) for s in scratch]
        + [pltpu.SMEM((8, 128), jnp.int32)]
        + [pltpu.VMEM(*s) for s in scratch2]
        + [pltpu.SemaphoreType.DMA((7,)), pltpu.SemaphoreType.DMA((NREMOTE,)), pltpu.SemaphoreType.DMA((NREMOTE,))],
        compiler_params=pltpu.CompilerParams(
            collective_id=0, has_side_effects=True, vmem_limit_bytes=60 * 2**20
        ),
        cost_estimate=pl.CostEstimate(flops=5_000_000_000, bytes_accessed=9_000_000, transcendentals=3_670_016),
        name="gist_backward",
    )(read_ids, read_counts, queries, grad_out, read_kv.reshape(ROWS, 2, 256), gist_states, kv_weight)
    return pl.pallas_call(
        write_out,
        out_shape=[jax.ShapeDtypeStruct(r.shape, r.dtype) for r in results],
        in_specs=[anywhere] * 3,
        out_specs=[anywhere] * 3,
        scratch_shapes=[pltpu.VMEM(r.shape, r.dtype) for r in results] + [pltpu.SemaphoreType.DMA((2, 6))],
        compiler_params=pltpu.CompilerParams(vmem_limit_bytes=62 * 2**20),
        cost_estimate=pl.CostEstimate(flops=0, bytes_accessed=2_500_000, transcendentals=0),
        name="write_out",
    )(*results)


def solution(mesh):
    placed = (
        P("span", "mp"),
        P("span", "mp"),
        P("span", None, None, "mp"),
        P("span", None),
        P("span", None),
        P("span", None),
        P(None, None, "mp"),
    )
    return jax.shard_map(
        body,
        mesh=mesh,
        in_specs=placed,
        out_specs=(P("span", "mp"), P("span", None, "mp"), P("span", "mp")),
        check_vma=False,
    )
```

```python
import jax
import jax.numpy as jnp
from jax import lax
from jax.experimental import pallas as pl
from jax.experimental.pallas import tpu as pltpu
from jax.sharding import PartitionSpec as P

HD = 128
SLOTS = 28
G = 32
LEN = 512
ROWS = SLOTS * G
NX, NZ, NY = 4, 8, 4
WIDTHS = (256, 256)
TILE = 128
SCALE = HD ** (-0.5)
NT = (((1,), (1,)), ((), ()))
NN = (((1,), (0,)), ((), ()))
MESH = pl.DeviceIdType.MESH
F32, BF16 = jnp.float32, jnp.bfloat16


def dot(a, b, dims=NN):
    return lax.dot_general(a, b, dims, preferred_element_type=F32)


def unmix():
    r = lax.broadcasted_iota(jnp.int32, (256, 256), 0)
    c = lax.broadcasted_iota(jnp.int32, (256, 256), 1)
    return jnp.where(c == jnp.where(r < 128, 2 * r, 2 * r - 255), 1.0, 0.0).astype(BF16)


GS = 0
Y = 7
BASE, PER = 10, 31
CORE, XA, XB, XC, ZR, AG, WX = 0, 4, 6, 8, 10, 17, 24
NREMOTE = BASE + 2 * PER


def kernel(
    ids, cnt, q_hbm, do_hbm, kv_hbm, gs_hbm, w_hbm,
    dq_ref, wg_ref, sg_ref,
    q_ref, do_ref, kv_ref, gs_ref, w_ref,
    k_s, v_s, dk_s, dv_s, ds_s, first_s, posv, pos,
    gsend, gsall, gst, wd, usend, ur,
    parts, sbuf, rbuf, xs, relay, xr, pz, zr, gg, ggall, wp, wsend, qr,
    lsem, ssem, rsem,
):
    span = lax.axis_index("span")
    y = lax.axis_index("mp")
    x, z, c = span // (NZ * 2), (span // 2) % NZ, span % 2

    def at(dx=0, dz=0, dc=0, dy=0):
        place = (((x + dx) % NX) * NZ + (z + dz) % NZ) * 2 + (c + dc) % 2
        return {"span": place, "mp": (y + dy) % NY}

    def remote(src, dst, k, to):
        return pltpu.make_async_remote_copy(
            src_ref=src, dst_ref=dst, send_sem=ssem.at[k], recv_sem=rsem.at[k],
            device_id=to, device_id_type=MESH,
        )

    sent, got = [], []

    def start(copy, *which):
        copy(*which).start()
        sent.append((copy, which))

    def arrived(copy, *which):
        copy(*which).wait_recv()
        got.append((copy, which))

    loads = [pltpu.make_async_copy(kv_hbm.reshape(2 * ROWS, 256), kv_ref, lsem.at[0])]
    for n, (i, o) in enumerate(((q_hbm, q_ref), (do_hbm, do_ref))):
        loads.append(pltpu.make_async_copy(i, o, lsem.at[1 + n]))
    loads.append(pltpu.make_async_copy(gs_hbm, gs_ref, lsem.at[3]))
    loads.append(pltpu.make_async_copy(w_hbm.reshape(8192, 256), w_ref, lsem.at[4]))
    for load in loads[:4]:
        load.start()

    peers = [at(dx=d, dc=k) for d in range(NX) for k in range(2) if d or k]
    peers += [at(dz=d) for d in range(1, NZ)] + [at(dy=d) for d in (1, 2, 3)]
    barrier = pltpu.get_barrier_semaphore()
    for peer in peers:
        pl.semaphore_signal(barrier, inc=1, device_id=peer, device_id_type=MESH)

    lane8 = lax.broadcasted_iota(jnp.int32, (8, 128), 1)
    where = jnp.full((8, 128), SLOTS, jnp.int32)
    for t in range(SLOTS):
        where = jnp.where(lane8 == ids[0, t], t, where)
    posv[...] = where
    to_smem = pltpu.make_async_copy(posv, pos, lsem.at[5])
    to_smem.start()
    for p, width in enumerate(WIDTHS):
        parts[p][SLOTS] = jnp.zeros((G, width), BF16)
    lane = lane8
    for b in range(7):
        first = LEN - cnt[0, 4 * b + 3]
        for j in (2, 1, 0):
            first = jnp.where(lane < 32 * (j + 1), LEN - cnt[0, 4 * b + j], first)
        first_s[:, b * 128 : (b + 1) * 128] = first
    dk_s[...] = jnp.zeros_like(dk_s)
    dv_s[...] = jnp.zeros_like(dv_s)

    loads[0].wait()
    pm = unmix()
    for b in range(7):
        blk = dot(pm, kv_ref[b * 256 : (b + 1) * 256, :]).astype(BF16)
        for h in range(2):
            k_s[h, b * 128 : (b + 1) * 128, :] = blk[:128, h * 128 : (h + 1) * 128]
            v_s[h, b * 128 : (b + 1) * 128, :] = blk[128:, h * 128 : (h + 1) * 128]

    def gs_copy(d):
        rows = pl.ds(pl.multiple_of(z * G, G), G)
        return remote(gsend.at[(z + d) % NZ], gsall.at[rows], GS + d - 1, at(dz=d))

    def gs_send():
        loads[3].wait()
        for zt in range(NZ):
            for xt in range(NX):
                col = (xt * NZ + zt) * 128
                gsend[zt, :, xt * 128 : (xt + 1) * 128] = gs_ref[:, col : col + 128]
        gsall[pl.ds(pl.multiple_of(z * G, G), G), :] = gsend[z]
        pl.semaphore_wait(barrier, len(peers))
        for d in (4, 3, 5, 2, 6, 1, 7):
            start(gs_copy, d)
        loads[4].start()

    loads[1].wait()
    loads[2].wait()

    def tile_rows(ref, h, t):
        tok = pl.ds(pl.multiple_of(t * TILE, TILE), TILE)
        return jnp.concatenate(
            [ref[tok, pl.ds(pl.multiple_of(h * 512 + g * 128, 128), 128)] for g in range(4)], axis=0
        )

    token = lax.broadcasted_iota(jnp.int32, (TILE, ROWS), 0)

    def half_tanh(h, t, qt):
        first = jnp.concatenate([first_s[...]] * (TILE // 8), axis=0)
        bias = jnp.where(token >= first - t * TILE, -0.5, -1e30).astype(F32)
        return jnp.tanh(dot(qt, k_s[h], NT) * (0.5 * SCALE) + jnp.concatenate([bias] * 4, axis=0))

    def attend(i):
        h, t = i // 4, i % 4
        qt, dt = tile_rows(q_ref, h, t), tile_rows(do_ref, h, t)
        u = half_tanh(h, t, qt)
        probs = (0.5 + 0.5 * u).astype(BF16)
        ds = (dot(dt, v_s[h], NT) * (1.0 - u * u)).astype(BF16)
        ds_s[i] = ds
        dv_s[h] += dot(dt.T, probs)
        dk_s[h] += dot(qt.T, ds)

    def finish_dq(i):
        h, t = i // 4, i % 4
        tok = pl.ds(pl.multiple_of(t * TILE, TILE), TILE)
        dq = (dot(ds_s[i], k_s[h]) * (0.25 * SCALE)).astype(BF16)
        for g in range(4):
            cols = pl.ds(pl.multiple_of(h * 512 + g * 128, 128), 128)
            dq_ref[tok, cols] = dq[g * 128 : (g + 1) * 128, :]

    def block(k):
        return pl.ds(pl.multiple_of(k * G, G), G)

    def core_copy(p, d):
        return remote(sbuf[p].at[d], rbuf[p].at[d], BASE + PER * p + CORE + d, at(dc=1))

    def core_send(p):
        key_part = (dk_s[p] * (0.25 * SCALE)).astype(BF16).T
        parts[p][:SLOTS, :, :128] = key_part.reshape(SLOTS, G, 128)
        value_part = dv_s[p].astype(BF16).T
        parts[p][:SLOTS, :, 128:] = value_part.reshape(SLOTS, G, 128)
        for d in (2, 1, 3, 0):
            def gather(zt, carry):
                slot = pos[0, (((x + d) % NX) * NZ + zt) * 2 + 1 - c]
                sbuf[p][d, block(zt), :] = parts[p][slot]
                return carry
            lax.fori_loop(0, NZ, gather, 0, unroll=True)
            start(core_copy, p, d)

    def pair_sum(p, d):
        arrived(core_copy, p, d)
        def add(zt, carry):
            slot = pos[0, (((x + d) % NX) * NZ + zt) * 2 + c]
            own = parts[p][slot].astype(F32)
            xs[p][d, block(zt), :] = (own + rbuf[p][d, block(zt), :].astype(F32)).astype(BF16)
            return carry
        lax.fori_loop(0, NZ, add, 0, unroll=True)

    LO, HI = pl.ds(0, 128), pl.ds(128, 128)

    def xa(p, n):
        rows = (LO, HI)[n]
        return remote(xs[p].at[2, rows], relay[p].at[n], BASE + PER * p + XA + n, at(dx=(1, 3)[n]))

    def xb(p, n):
        d, rows = ((1, HI), (3, LO))[n]
        return remote(xs[p].at[d, rows], xr[p].at[n, rows], BASE + PER * p + XB + n, at(dx=d))

    def xc(p, n):
        d, rows = ((1, LO), (3, HI))[n]
        return remote(xs[p].at[d, rows], xr[p].at[n, rows], BASE + PER * p + XC + n, at(dx=d))

    def x_first(p):
        pair_sum(p, 2)
        start(xa, p, 0)
        start(xa, p, 1)
        pair_sum(p, 1)
        start(xb, p, 0)
        pair_sum(p, 3)
        start(xb, p, 1)
        pair_sum(p, 0)

    def x_second(p):
        for n in range(2):
            d, rows = ((1, slice(0, 128)), (3, slice(128, 256)))[n]
            arrived(xa, p, n)
            xs[p][d, rows, :] = (xs[p][d, rows, :].astype(F32) + relay[p][n].astype(F32)).astype(BF16)
            start(xc, p, n)

    def z_copy(p, d):
        return remote(pz[p].at[block((z + d) % NZ)], zr[p].at[d - 1], BASE + PER * p + ZR + d - 1, at(dz=d))

    def z_send(p):
        for n in range(2):
            arrived(xb, p, n)
            arrived(xc, p, n)
        pz[p][...] = (xs[p][0].astype(F32) + xr[p][0].astype(F32) + xr[p][1].astype(F32)).astype(BF16)
        for d in (4, 3, 5, 2, 6, 1, 7):
            start(z_copy, p, d)

    def ag_copy(p, d):
        return remote(gg[p], ggall[p].at[block(z)], BASE + PER * p + AG + d - 1, at(dz=d))

    def z_sum(p):
        total = pz[p][block(z), :].astype(F32)
        for d in range(1, NZ):
            arrived(z_copy, p, d)
            total += zr[p][d - 1].astype(F32)
        gg[p][...] = total.astype(BF16)
        for d in (4, 3, 5, 2, 6, 1, 7):
            start(ag_copy, p, d)
        ggall[p][block(z), :] = gg[p][...]

    def rows_of(xt, cc):
        return pl.ds(pl.multiple_of(xt * 128 + cc * 64, 64), 64)

    def w_copy(p, d, k):
        n = 2 * d + k - 1
        rows = rows_of((x + d) % NX, (c + k) % 2)
        return remote(wsend[p].at[rows], qr[p].at[n], BASE + PER * p + WX + n, at(dx=d, dc=k))

    W_ORDER = ((2, 0), (2, 1), (1, 0), (3, 0), (1, 1), (3, 1), (0, 1))

    def w_send(p):
        for d in range(1, NZ):
            arrived(ag_copy, p, d)
        wp[p][...] = dot(gst[...], ggall[p][...])
        wsend[p][...] = wp[p][...].astype(BF16)
        for d, k in W_ORDER:
            start(w_copy, p, d, k)

    def w_last(p):
        total = wp[p][rows_of(x, c), :]
        for d, k in W_ORDER:
            arrived(w_copy, p, d, k)
            total += qr[p][2 * d + k - 1].astype(F32)
        for s in range(2):
            wg_ref[:, s, p * 128 : (p + 1) * 128] = total[:, s * 128 : (s + 1) * 128]

    def y_copy(d):
        return remote(usend.at[(y + d) % NY], ur.at[d - 1], Y + d - 1, at(dy=d))

    def state_send():
        for yt in range(NY):
            rows = slice(yt * 1024, (yt + 1) * 1024)
            part = jnp.zeros((G, 1024), F32)
            for s in range(2):
                left = jnp.concatenate([gg[p][:, s * 128 : (s + 1) * 128] for p in range(2)], axis=1)
                part += dot(left, wd[s, rows, :], NT)
            usend[yt] = part.astype(BF16)
        for d in (2, 1, 3):
            start(y_copy, d)

    def state_last():
        total = usend[y].astype(F32)
        for d in (1, 2, 3):
            arrived(y_copy, d)
            total += ur[d - 1].astype(F32)
        sg_ref[...] = total.astype(BF16)

    def dq_steps(lo, hi):
        lax.fori_loop(lo, hi, lambda i, carry: (finish_dq(i), carry)[1], 0)

    def split_w(lo, hi):
        def one(b, carry):
            blk = dot(pm, w_ref[pl.ds(pl.multiple_of(b * 256, 256), 256), :]).astype(BF16)
            rows = pl.ds(pl.multiple_of(b * 128, 128), 128)
            wd[0, rows, :] = blk[:128]
            wd[1, rows, :] = blk[128:]
            return carry

        lax.fori_loop(lo, hi, one, 0)

    to_smem.wait()

    def loop(i, carry):
        attend(i)

        @pl.when(i == 0)
        def _():
            gs_send()

        @pl.when(i == 3)
        def _():
            core_send(0)

        @pl.when(i == 5)
        def _():
            x_first(0)

        @pl.when(i == 7)
        def _():
            core_send(1)
            x_second(0)

        return carry

    lax.fori_loop(0, 8, loop, 0)

    loads[4].wait()
    split_w(0, 8)
    x_first(1)
    dq_steps(0, 4)
    z_send(0)
    split_w(8, 16)
    x_second(1)
    split_w(16, 32)
    for d in range(1, NZ):
        arrived(gs_copy, d)
    gst[...] = gsall[...].T
    z_send(1)
    z_sum(0)
    dq_steps(4, 8)
    z_sum(1)
    w_send(0)
    state_send()
    w_send(1)
    w_last(0)
    state_last()
    w_last(1)

    for copy, which in sent:
        copy(*which).wait_send()


def write_out(a, b, c, a_out, b_out, c_out, a_s, b_s, c_s, sem):
    moves = [(a.at[pl.ds(r, 128)], a_s.at[pl.ds(r, 128)], a_out.at[pl.ds(r, 128)]) for r in range(0, 512, 128)]
    moves += [(b, b_s, b_out), (c, c_s, c_out)]
    reads = [pltpu.make_async_copy(i, s, sem.at[0, n]) for n, (i, s, _) in enumerate(moves)]
    writes = [pltpu.make_async_copy(s, o, sem.at[1, n]) for n, (_, s, o) in enumerate(moves)]
    for read in reads:
        read.start()
    for read, write in zip(reads, writes):
        read.wait()
        write.start()
    for write in writes:
        write.wait()


def body(queries, grad_out, read_kv, read_ids, read_counts, gist_states, kv_weight):
    smem, vmem, anywhere = (pl.BlockSpec(memory_space=m) for m in (pltpu.SMEM, pltpu.VMEM, pl.ANY))
    scratch = [
        ((512, 1024), BF16), ((512, 1024), BF16), ((2 * ROWS, 256), BF16), ((G, 4096), BF16), ((8192, 256), BF16),
        ((2, ROWS, 128), BF16), ((2, ROWS, 128), BF16), ((2, 128, ROWS), F32), ((2, 128, ROWS), F32),
        ((8, 512, ROWS), BF16), ((8, ROWS), jnp.int32), ((8, 128), jnp.int32),
    ]
    scratch2 = [
        ((NZ, G, 512), BF16), ((256, 512), BF16), ((512, 256), BF16), ((2, 4096, 256), BF16),
        ((NY, G, 1024), BF16), ((3, G, 1024), BF16),
    ]
    by_piece = [
        ((SLOTS + 1, G), BF16), ((4, 256), BF16), ((4, 256), BF16), ((4, 256), BF16),
        ((2, 128), BF16), ((2, 256), BF16), ((256,), BF16), ((7, G), BF16), ((G,), BF16), ((256,), BF16),
        ((512,), F32), ((512,), BF16), ((7, 64), BF16),
    ]
    results = pl.pallas_call(
        kernel,
        out_shape=(
            jax.ShapeDtypeStruct((512, 1024), BF16),
            jax.ShapeDtypeStruct((64, 2, 256), F32),
            jax.ShapeDtypeStruct((G, 1024), BF16),
        ),
        in_specs=[smem, smem] + [anywhere] * 5,
        out_specs=(vmem, vmem, vmem),
        scratch_shapes=[pltpu.VMEM(*s) for s in scratch]
        + [pltpu.SMEM((8, 128), jnp.int32)]
        + [pltpu.VMEM(*s) for s in scratch2]
        + [tuple(pltpu.VMEM(shape + (w,), kind) for w in WIDTHS) for shape, kind in by_piece]
        + [pltpu.SemaphoreType.DMA((7,)), pltpu.SemaphoreType.DMA((NREMOTE,)), pltpu.SemaphoreType.DMA((NREMOTE,))],
        compiler_params=pltpu.CompilerParams(
            collective_id=0, has_side_effects=True, vmem_limit_bytes=60 * 2**20
        ),
        cost_estimate=pl.CostEstimate(flops=5_000_000_000, bytes_accessed=9_000_000, transcendentals=3_670_016),
        name="gist_backward",
    )(read_ids, read_counts, queries, grad_out, read_kv.reshape(ROWS, 2, 256), gist_states, kv_weight)
    return pl.pallas_call(
        write_out,
        out_shape=[jax.ShapeDtypeStruct(r.shape, r.dtype) for r in results],
        in_specs=[anywhere] * 3,
        out_specs=[anywhere] * 3,
        scratch_shapes=[pltpu.VMEM(r.shape, r.dtype) for r in results] + [pltpu.SemaphoreType.DMA((2, 6))],
        compiler_params=pltpu.CompilerParams(vmem_limit_bytes=62 * 2**20),
        cost_estimate=pl.CostEstimate(flops=0, bytes_accessed=2_500_000, transcendentals=0),
        name="write_out",
    )(*results)


def solution(mesh):
    placed = (
        P("span", "mp"),
        P("span", "mp"),
        P("span", None, None, "mp"),
        P("span", None),
        P("span", None),
        P("span", None),
        P(None, None, "mp"),
    )
    return jax.shard_map(
        body,
        mesh=mesh,
        in_specs=placed,
        out_specs=(P("span", "mp"), P("span", None, "mp"), P("span", "mp")),
        check_vma=False,
    )
```

```python
import jax
import jax.numpy as jnp
from jax import lax
from jax.experimental import pallas as pl
from jax.experimental.pallas import tpu as pltpu
from jax.sharding import PartitionSpec as P

HD = 128
SLOTS = 28
G = 32
LEN = 512
ROWS = SLOTS * G
NX, NZ, NY = 4, 8, 4
WIDTHS = (256, 256)
TILE = 128
SCALE = HD ** (-0.5)
NT = (((1,), (1,)), ((), ()))
NN = (((1,), (0,)), ((), ()))
MESH = pl.DeviceIdType.MESH
F32, BF16 = jnp.float32, jnp.bfloat16


def dot(a, b, dims=NN):
    return lax.dot_general(a, b, dims, preferred_element_type=F32)


def unmix():
    r = lax.broadcasted_iota(jnp.int32, (256, 256), 0)
    c = lax.broadcasted_iota(jnp.int32, (256, 256), 1)
    return jnp.where(c == jnp.where(r < 128, 2 * r, 2 * r - 255), 1.0, 0.0).astype(BF16)


GS = 0
Y = 7
BASE, PER = 10, 31
CORE, XA, XB, XC, ZR, AG, WX = 0, 4, 6, 8, 10, 17, 24
NREMOTE = BASE + 2 * PER


def kernel(
    ids, cnt, q_hbm, do_hbm, kv_hbm, gs_hbm, w_hbm,
    dq_ref, wg_ref, sg_ref,
    q_ref, do_ref, kv_ref, gs_ref, w_ref,
    k_s, v_s, dk_s, dv_s, ds_s, first_s, posv, pos,
    gsend, gsall, gst, wd, usend, ur,
    parts, sbuf, rbuf, xs, relay, xr, pz, zr, gg, ggall, wp, wsend, qr,
    lsem, ssem, rsem,
):
    span = lax.axis_index("span")
    y = lax.axis_index("mp")
    x, z, c = span // (NZ * 2), (span // 2) % NZ, span % 2

    def at(dx=0, dz=0, dc=0, dy=0):
        place = (((x + dx) % NX) * NZ + (z + dz) % NZ) * 2 + (c + dc) % 2
        return {"span": place, "mp": (y + dy) % NY}

    def remote(src, dst, k, to):
        return pltpu.make_async_remote_copy(
            src_ref=src, dst_ref=dst, send_sem=ssem.at[k], recv_sem=rsem.at[k],
            device_id=to, device_id_type=MESH,
        )

    sent, got = [], []

    def start(copy, *which):
        copy(*which).start()
        sent.append((copy, which))

    def arrived(copy, *which):
        copy(*which).wait_recv()
        got.append((copy, which))

    loads = [pltpu.make_async_copy(kv_hbm.reshape(2 * ROWS, 256), kv_ref, lsem.at[0])]
    for n, (i, o) in enumerate(((q_hbm, q_ref), (do_hbm, do_ref))):
        loads.append(pltpu.make_async_copy(i, o, lsem.at[1 + n]))
    loads.append(pltpu.make_async_copy(gs_hbm, gs_ref, lsem.at[3]))
    loads.append(pltpu.make_async_copy(w_hbm.reshape(8192, 256), w_ref, lsem.at[4]))
    for load in loads[:4]:
        load.start()

    peers = [at(dx=d, dc=k) for d in range(NX) for k in range(2) if d or k]
    peers += [at(dz=d) for d in range(1, NZ)] + [at(dy=d) for d in (1, 2, 3)]
    barrier = pltpu.get_barrier_semaphore()
    for peer in peers:
        pl.semaphore_signal(barrier, inc=1, device_id=peer, device_id_type=MESH)

    lane8 = lax.broadcasted_iota(jnp.int32, (8, 128), 1)
    where = jnp.full((8, 128), SLOTS, jnp.int32)
    for t in range(SLOTS):
        where = jnp.where(lane8 == ids[0, t], t, where)
    posv[...] = where
    to_smem = pltpu.make_async_copy(posv, pos, lsem.at[5])
    to_smem.start()
    for p, width in enumerate(WIDTHS):
        parts[p][SLOTS] = jnp.zeros((G, width), BF16)
    lane = lane8
    for b in range(7):
        first = LEN - cnt[0, 4 * b + 3]
        for j in (2, 1, 0):
            first = jnp.where(lane < 32 * (j + 1), LEN - cnt[0, 4 * b + j], first)
        first_s[:, b * 128 : (b + 1) * 128] = first
    dk_s[...] = jnp.zeros_like(dk_s)
    dv_s[...] = jnp.zeros_like(dv_s)

    loads[0].wait()
    pm = unmix()
    for b in range(7):
        blk = dot(pm, kv_ref[b * 256 : (b + 1) * 256, :]).astype(BF16)
        for h in range(2):
            k_s[h, b * 128 : (b + 1) * 128, :] = blk[:128, h * 128 : (h + 1) * 128]
            v_s[h, b * 128 : (b + 1) * 128, :] = blk[128:, h * 128 : (h + 1) * 128]

    def gs_copy(d):
        rows = pl.ds(pl.multiple_of(z * G, G), G)
        return remote(gsend.at[(z + d) % NZ], gsall.at[rows], GS + d - 1, at(dz=d))

    def gs_send():
        loads[3].wait()
        for zt in range(NZ):
            for xt in range(NX):
                col = (xt * NZ + zt) * 128
                gsend[zt, :, xt * 128 : (xt + 1) * 128] = gs_ref[:, col : col + 128]
        gsall[pl.ds(pl.multiple_of(z * G, G), G), :] = gsend[z]
        pl.semaphore_wait(barrier, len(peers))
        for d in (4, 3, 5, 2, 6, 1, 7):
            start(gs_copy, d)
        loads[4].start()

    loads[1].wait()
    loads[2].wait()

    def tile_rows(ref, h, t):
        tok = pl.ds(pl.multiple_of(t * TILE, TILE), TILE)
        return jnp.concatenate(
            [ref[tok, pl.ds(pl.multiple_of(h * 512 + g * 128, 128), 128)] for g in range(4)], axis=0
        )

    token = lax.broadcasted_iota(jnp.int32, (TILE, ROWS), 0)

    def half_tanh(h, t, qt):
        first = jnp.concatenate([first_s[...]] * (TILE // 8), axis=0)
        bias = jnp.where(token >= first - t * TILE, -0.5, -1e30).astype(F32)
        return jnp.tanh(dot(qt, k_s[h], NT) * (0.5 * SCALE) + jnp.concatenate([bias] * 4, axis=0))

    def attend(i):
        h, t = i // 4, i % 4
        qt, dt = tile_rows(q_ref, h, t), tile_rows(do_ref, h, t)
        u = half_tanh(h, t, qt)
        probs = (0.5 + 0.5 * u).astype(BF16)
        ds = (dot(dt, v_s[h], NT) * (1.0 - u * u)).astype(BF16)
        ds_s[i] = ds
        dv_s[h] += dot(dt.T, probs)
        dk_s[h] += dot(qt.T, ds)

    def finish_dq(i):
        h, t = i // 4, i % 4
        tok = pl.ds(pl.multiple_of(t * TILE, TILE), TILE)
        dq = (dot(ds_s[i], k_s[h]) * (0.25 * SCALE)).astype(BF16)
        for g in range(4):
            cols = pl.ds(pl.multiple_of(h * 512 + g * 128, 128), 128)
            dq_ref[tok, cols] = dq[g * 128 : (g + 1) * 128, :]

    def block(k):
        return pl.ds(pl.multiple_of(k * G, G), G)

    def core_copy(p, d):
        return remote(sbuf[p].at[d], rbuf[p].at[d], BASE + PER * p + CORE + d, at(dc=1))

    def core_send(p):
        key_part = (dk_s[p] * (0.25 * SCALE)).astype(BF16).T
        parts[p][:SLOTS, :, :128] = key_part.reshape(SLOTS, G, 128)
        value_part = dv_s[p].astype(BF16).T
        parts[p][:SLOTS, :, 128:] = value_part.reshape(SLOTS, G, 128)
        for d in (2, 1, 3, 0):
            def gather(zt, carry):
                slot = pos[0, (((x + d) % NX) * NZ + zt) * 2 + 1 - c]
                sbuf[p][d, block(zt), :] = parts[p][slot]
                return carry
            lax.fori_loop(0, NZ, gather, 0, unroll=True)
            start(core_copy, p, d)

    def pair_sum(p, d):
        arrived(core_copy, p, d)
        def add(zt, carry):
            slot = pos[0, (((x + d) % NX) * NZ + zt) * 2 + c]
            own = parts[p][slot].astype(F32)
            xs[p][d, block(zt), :] = (own + rbuf[p][d, block(zt), :].astype(F32)).astype(BF16)
            return carry
        lax.fori_loop(0, NZ, add, 0, unroll=True)

    LO, HI = pl.ds(0, 128), pl.ds(128, 128)

    def xa(p, n):
        rows = (LO, HI)[n]
        return remote(xs[p].at[2, rows], relay[p].at[n], BASE + PER * p + XA + n, at(dx=(1, 3)[n]))

    def xb(p, n):
        d, rows = ((1, HI), (3, LO))[n]
        return remote(xs[p].at[d, rows], xr[p].at[n, rows], BASE + PER * p + XB + n, at(dx=d))

    def xc(p, n):
        d, rows = ((1, LO), (3, HI))[n]
        return remote(xs[p].at[d, rows], xr[p].at[n, rows], BASE + PER * p + XC + n, at(dx=d))

    def x_first(p):
        pair_sum(p, 2)
        start(xa, p, 0)
        start(xa, p, 1)
        pair_sum(p, 1)
        start(xb, p, 0)
        pair_sum(p, 3)
        start(xb, p, 1)
        pair_sum(p, 0)

    def x_second(p):
        for n in range(2):
            d, rows = ((1, slice(0, 128)), (3, slice(128, 256)))[n]
            arrived(xa, p, n)
            xs[p][d, rows, :] = (xs[p][d, rows, :].astype(F32) + relay[p][n].astype(F32)).astype(BF16)
            start(xc, p, n)

    def z_copy(p, d):
        return remote(pz[p].at[block((z + d) % NZ)], zr[p].at[d - 1], BASE + PER * p + ZR + d - 1, at(dz=d))

    def z_send(p):
        for n in range(2):
            arrived(xb, p, n)
            arrived(xc, p, n)
        pz[p][...] = (xs[p][0].astype(F32) + xr[p][0].astype(F32) + xr[p][1].astype(F32)).astype(BF16)
        for d in (4, 3, 5, 2, 6, 1, 7):
            start(z_copy, p, d)

    def ag_copy(p, d):
        return remote(gg[p], ggall[p].at[block(z)], BASE + PER * p + AG + d - 1, at(dz=d))

    def z_sum(p):
        total = pz[p][block(z), :].astype(F32)
        for d in range(1, NZ):
            arrived(z_copy, p, d)
            total += zr[p][d - 1].astype(F32)
        gg[p][...] = total.astype(BF16)
        for d in (4, 3, 5, 2, 6, 1, 7):
            start(ag_copy, p, d)
        ggall[p][block(z), :] = gg[p][...]

    def rows_of(xt, cc):
        return pl.ds(pl.multiple_of(xt * 128 + cc * 64, 64), 64)

    def w_copy(p, d, k):
        n = 2 * d + k - 1
        rows = rows_of((x + d) % NX, (c + k) % 2)
        return remote(wsend[p].at[rows], qr[p].at[n], BASE + PER * p + WX + n, at(dx=d, dc=k))

    W_ORDER = ((2, 0), (2, 1), (1, 0), (3, 0), (1, 1), (3, 1), (0, 1))

    def w_send(p):
        for d in range(1, NZ):
            arrived(ag_copy, p, d)
        wp[p][...] = dot(gst[...], ggall[p][...])
        wsend[p][...] = wp[p][...].astype(BF16)
        for d, k in W_ORDER:
            start(w_copy, p, d, k)

    def w_last(p):
        total = wp[p][rows_of(x, c), :]
        for d, k in W_ORDER:
            arrived(w_copy, p, d, k)
            total += qr[p][2 * d + k - 1].astype(F32)
        for s in range(2):
            wg_ref[:, s, p * 128 : (p + 1) * 128] = total[:, s * 128 : (s + 1) * 128]

    def y_copy(d):
        return remote(usend.at[(y + d) % NY], ur.at[d - 1], Y + d - 1, at(dy=d))

    def state_send():
        for yt in range(NY):
            rows = slice(yt * 1024, (yt + 1) * 1024)
            part = jnp.zeros((G, 1024), F32)
            for s in range(2):
                left = jnp.concatenate([gg[p][:, s * 128 : (s + 1) * 128] for p in range(2)], axis=1)
                part += dot(left, wd[s, rows, :], NT)
            usend[yt] = part.astype(BF16)
        for d in (2, 1, 3):
            start(y_copy, d)

    def state_last():
        total = usend[y].astype(F32)
        for d in (1, 2, 3):
            arrived(y_copy, d)
            total += ur[d - 1].astype(F32)
        sg_ref[...] = total.astype(BF16)

    def dq_steps(lo, hi):
        lax.fori_loop(lo, hi, lambda i, carry: (finish_dq(i), carry)[1], 0)

    def split_w(lo, hi):
        def one(b, carry):
            blk = dot(pm, w_ref[pl.ds(pl.multiple_of(b * 256, 256), 256), :]).astype(BF16)
            rows = pl.ds(pl.multiple_of(b * 128, 128), 128)
            wd[0, rows, :] = blk[:128]
            wd[1, rows, :] = blk[128:]
            return carry

        lax.fori_loop(lo, hi, one, 0)

    to_smem.wait()

    def loop(i, carry):
        attend(i)

        @pl.when(i == 1)
        def _():
            gs_send()

        @pl.when(i == 3)
        def _():
            core_send(0)

        @pl.when(i == 5)
        def _():
            x_first(0)

        @pl.when(i == 7)
        def _():
            core_send(1)
            x_second(0)

        return carry

    lax.fori_loop(0, 8, loop, 0)

    loads[4].wait()
    split_w(0, 8)
    x_first(1)
    dq_steps(0, 4)
    z_send(0)
    split_w(8, 16)
    x_second(1)
    split_w(16, 32)
    for d in range(1, NZ):
        arrived(gs_copy, d)
    gst[...] = gsall[...].T
    z_send(1)
    z_sum(0)
    dq_steps(4, 8)
    z_sum(1)
    state_send()
    w_send(0)
    w_send(1)
    w_last(0)
    state_last()
    w_last(1)

    for copy, which in sent:
        copy(*which).wait_send()


def write_out(a, b, c, a_out, b_out, c_out, a_s, b_s, c_s, sem):
    moves = [(a.at[pl.ds(r, 128)], a_s.at[pl.ds(r, 128)], a_out.at[pl.ds(r, 128)]) for r in range(0, 512, 128)]
    moves += [(b, b_s, b_out), (c, c_s, c_out)]
    reads = [pltpu.make_async_copy(i, s, sem.at[0, n]) for n, (i, s, _) in enumerate(moves)]
    writes = [pltpu.make_async_copy(s, o, sem.at[1, n]) for n, (_, s, o) in enumerate(moves)]
    for read in reads:
        read.start()
    for read, write in zip(reads, writes):
        read.wait()
        write.start()
    for write in writes:
        write.wait()


def body(queries, grad_out, read_kv, read_ids, read_counts, gist_states, kv_weight):
    smem, vmem, anywhere = (pl.BlockSpec(memory_space=m) for m in (pltpu.SMEM, pltpu.VMEM, pl.ANY))
    scratch = [
        ((512, 1024), BF16), ((512, 1024), BF16), ((2 * ROWS, 256), BF16), ((G, 4096), BF16), ((8192, 256), BF16),
        ((2, ROWS, 128), BF16), ((2, ROWS, 128), BF16), ((2, 128, ROWS), F32), ((2, 128, ROWS), F32),
        ((8, 512, ROWS), BF16), ((8, ROWS), jnp.int32), ((8, 128), jnp.int32),
    ]
    scratch2 = [
        ((NZ, G, 512), BF16), ((256, 512), BF16), ((512, 256), BF16), ((2, 4096, 256), BF16),
        ((NY, G, 1024), BF16), ((3, G, 1024), BF16),
    ]
    by_piece = [
        ((SLOTS + 1, G), BF16), ((4, 256), BF16), ((4, 256), BF16), ((4, 256), BF16),
        ((2, 128), BF16), ((2, 256), BF16), ((256,), BF16), ((7, G), BF16), ((G,), BF16), ((256,), BF16),
        ((512,), F32), ((512,), BF16), ((7, 64), BF16),
    ]
    results = pl.pallas_call(
        kernel,
        out_shape=(
            jax.ShapeDtypeStruct((512, 1024), BF16),
            jax.ShapeDtypeStruct((64, 2, 256), F32),
            jax.ShapeDtypeStruct((G, 1024), BF16),
        ),
        in_specs=[smem, smem] + [anywhere] * 5,
        out_specs=(vmem, vmem, vmem),
        scratch_shapes=[pltpu.VMEM(*s) for s in scratch]
        + [pltpu.SMEM((8, 128), jnp.int32)]
        + [pltpu.VMEM(*s) for s in scratch2]
        + [tuple(pltpu.VMEM(shape + (w,), kind) for w in WIDTHS) for shape, kind in by_piece]
        + [pltpu.SemaphoreType.DMA((7,)), pltpu.SemaphoreType.DMA((NREMOTE,)), pltpu.SemaphoreType.DMA((NREMOTE,))],
        compiler_params=pltpu.CompilerParams(
            collective_id=0, has_side_effects=True, vmem_limit_bytes=60 * 2**20
        ),
        cost_estimate=pl.CostEstimate(flops=5_000_000_000, bytes_accessed=9_000_000, transcendentals=3_670_016),
        name="gist_backward",
    )(read_ids, read_counts, queries, grad_out, read_kv.reshape(ROWS, 2, 256), gist_states, kv_weight)
    return pl.pallas_call(
        write_out,
        out_shape=[jax.ShapeDtypeStruct(r.shape, r.dtype) for r in results],
        in_specs=[anywhere] * 3,
        out_specs=[anywhere] * 3,
        scratch_shapes=[pltpu.VMEM(r.shape, r.dtype) for r in results] + [pltpu.SemaphoreType.DMA((2, 6))],
        compiler_params=pltpu.CompilerParams(vmem_limit_bytes=62 * 2**20),
        cost_estimate=pl.CostEstimate(flops=0, bytes_accessed=2_500_000, transcendentals=0),
        name="write_out",
    )(*results)


def solution(mesh):
    placed = (
        P("span", "mp"),
        P("span", "mp"),
        P("span", None, None, "mp"),
        P("span", None),
        P("span", None),
        P("span", None),
        P(None, None, "mp"),
    )
    return jax.shard_map(
        body,
        mesh=mesh,
        in_specs=placed,
        out_specs=(P("span", "mp"), P("span", None, "mp"), P("span", "mp")),
        check_vma=False,
    )
```
